256 devices in a mesh: shot: 16 (over y, x_hi, core), slab: 16 (over x_lo, z).
Axes of the slice: x: 4 (x_hi: 2, x_lo: 2; x = x_hi * 2 + x_lo), y: 4, z: 8, core: 2. Of those that a mesh axis runs over, the one named last changes fastest.
Arguments:
- pressure_old: float32 [16, 640, 32, 128], P('shot', 'slab'), may hold values from -6 to 6
- pressure_now: float32 [16, 640, 32, 128], P('shot', 'slab'), may hold values from -6 to 6
- adjoint_later: float32 [16, 640, 32, 128], P('shot', 'slab'), may hold values from -6 to 6
- adjoint_now: float32 [16, 640, 32, 128], P('shot', 'slab'), may hold values from -6 to 6
- stiffness: float32 [640, 32, 128], P('slab'), may hold values from 0.02 to 0.12
- buoyancy: float32 [640, 32, 128], P('slab'), may hold values from 0.5 to 1.5
- traces: float32 [16, 4096, 2048], P('shot', 'slab'), may hold values from -6 to 6
- owner_slab: int32 [16, 4096, 1], P('shot', 'slab'), may hold values from 0 to 15; in each aligned block of 256 rows (0 to 255, 256 to 511, ..., all dimensions but the last counted through in order) at most 32 rows name the same one
- depth_plane: int32 [16, 4096], P('shot', 'slab'), may hold values from 0 to 39
- station_cell: int32 [16, 4096], P('shot', 'slab'), may hold values from 0 to 4095
- resampler: float32 [2, 2048], replicated, may hold values from -3 to 3
Outputs:
- gradient: float32 [640, 32, 128], P('slab', 'shot')
- adjoint_field: float32 [16, 640, 32, 128], P('shot', 'slab')
The draws below stay inside these ranges and needn't reach their ends.
Inputs may be any that keep to these rules, and one draw needn't show every extreme that they name: `owner_slab`: within each shot, among the 256 rows of each aligned block of rows, at most 32 name the same owner slab, a bound that some block reaches.
All inputs are finite; a program needn't handle non-finite values.
Results may differ from the reference program's by a relative error of at most 0.0003.
Values sent between devices are 32-bit elements; how exact they have to be, the bound alone decides.
A program may use at most 128 MiB of HBM per device.

```python
import math
import jax
import jax.numpy as jnp
import numpy as np
from jax import lax

PLANES = 40
NX = 32
NY = 128
SAMPLES = 2048
RB = 256
CAP = 32
SHOTS = 16
NZ = 640
RECV = 4096
N_SLAB = 16


def touch_ends(drawn, stream_key, low, high):
    extent = drawn.shape
    spot = [jax.random.randint(jax.random.fold_in(stream_key, axis), (), 0, extent[axis]) for axis in range(len(extent))]
    drawn = drawn.at[tuple(spot)].set(low)
    longest = extent.index(max(extent))
    spot[longest] = (spot[longest] + 1) % extent[longest]
    return drawn.at[tuple(spot)].set(high)


def spiked(values, stream_key, source, target, shards_of, factor):
    owner, partner = [(jnp.arange(values.shape[dim]) // (values.shape[dim] // shards_of)).reshape([-1 if axis == dim else 1 for axis in range(values.ndim)]) for dim in (source, target)]
    chosen = jax.random.permutation(stream_key, shards_of)[partner]
    strong = (owner == chosen) | (owner == (partner + shards_of // 2) % shards_of)
    return jnp.where(strong, factor * values, values)


def steps_of(rng, shape, pieces, low, largest):
    def one(axis_at, parts):
        draws = jax.random.uniform(jax.random.fold_in(jax.random.fold_in(rng, 6), axis_at), (parts,), jnp.float32, low / len(pieces), largest / len(pieces))
        return jnp.repeat(jnp.exp(draws), shape[axis_at] // parts).reshape((-1,) + (1,) * (len(shape) - axis_at - 1))

    factor_of = one(*pieces[0])
    for cut in pieces[1:]:
        factor_of = factor_of * one(*cut)
    return factor_of


def deal_out(rng, own, number, rows, number_of, top, limit, skew):
    sequence = jax.random.permutation(rng, number_of)
    heavy_load, ordinary = portions_of(number_of, rows * top, limit, skew, True), portions_of(number_of, rows * top, limit, skew, False)
    places = jnp.arange(number_of)

    def named(lengths, offset_by):
        used = int((lengths > 0).sum())
        fixed = max(1, used // 4)
        moved = fixed + (places - fixed + offset_by * (used - fixed)) % max(1, number_of - fixed)
        return jnp.zeros((number_of,), jnp.int32).at[sequence[jnp.where(places < fixed, places, moved)]].set(jnp.asarray(lengths, jnp.int32))

    lengths = jnp.where(number % 4 == 0, named(heavy_load, number // 4), named(ordinary, number - number // 4 - 1))
    mixed = jax.random.permutation(jax.random.fold_in(own, 3), number_of)
    source_of, taker = mixed[0:number_of // 2 * 2:2], mixed[1:number_of // 2 * 2:2]
    room = jnp.minimum(lengths[source_of] - 1, limit - lengths[taker]) // 2
    room = jnp.where((source_of == sequence[0]) | (taker == sequence[0]) | (lengths[taker] == 0), 0, jnp.maximum(room, 0))
    moved = jax.random.randint(jax.random.fold_in(own, 4), (number_of // 2,), 0, 1 << 20) % (room + 1)
    lengths = lengths.at[source_of].add(-moved).at[taker].add(moved)
    items = jnp.searchsorted(jnp.cumsum(lengths), jnp.arange(rows * top), side="right").astype(jnp.int32)
    table = items.reshape(top, rows).T
    table = table[jax.random.permutation(jax.random.fold_in(own, 1), rows)]
    offset_by = jax.random.randint(jax.random.fold_in(own, 2), (rows, 1), 0, top)
    return jnp.take_along_axis(table, (jnp.arange(top)[None, :] + offset_by) % top, axis=1)


def portions_of(number_of, total, reach, lean, full):
    loads = [(1 << 20) // math.isqrt(grade ** lean) + 1 for grade in range(1, number_of + 1)]
    largest = reach if full else min(reach, max(-(-total // number_of), total * loads[0] // sum(loads)))
    least = 1 if total - largest >= number_of - 1 else 0
    given, rest = [largest] + [least] * (number_of - 1), total - largest - least * (number_of - 1)
    while rest > 0:
        movable = [i for i in range(1, number_of) if given[i] < largest] or [i for i in range(1, number_of) if given[i] < reach]
        mass, budget = sum([loads[i] for i in movable]), rest
        for i in movable:
            more = min(reach - given[i], max(1, budget * loads[i] // mass), rest)
            given[i] = given[i] + more
            rest = rest - more
    return np.array(given)


def bell_draw(own_key, extent, spread, bound, shards=(), held_as=jnp.bfloat16):
    drawn = spread * jax.random.normal(own_key, extent, jnp.float32)
    if shards:
        drawn = drawn * steps_of(own_key, extent, shards, -0.22, 0.18)
    return jnp.clip(drawn, -bound, bound).astype(held_as)


def heavy_noise(stream_key, shape, spread, limit, cuts, heavy, kind=jnp.bfloat16):
    drawn = spread * jax.random.normal(stream_key, shape, jnp.float32)
    if cuts:
        drawn = drawn * steps_of(stream_key, shape, cuts, -0.22, 0.18)
    return jnp.clip(spiked(drawn, jax.random.fold_in(stream_key, 3), *heavy), -limit, limit).astype(kind)


def setup_inputs(seed: int = 0) -> dict:
    splits = jax.random.split(jax.random.key(seed), 12)
    pressure_old = bell_draw(splits[0], (SHOTS, NZ, NX, NY), 1.0, 6.0, ((0, 16), (1, 16)), jnp.float32)
    pressure_now = bell_draw(splits[1], (SHOTS, NZ, NX, NY), 1.0, 6.0, ((0, 16), (1, 16)), jnp.float32)
    adjoint_later = bell_draw(splits[2], (SHOTS, NZ, NX, NY), 1.0, 6.0, ((0, 16), (1, 16)), jnp.float32)
    adjoint_now = heavy_noise(splits[3], (SHOTS, NZ, NX, NY), 1.0, 6.0, ((0, 16), (1, 16)), (0, 2, 16, 2.0), jnp.float32)
    stiffness = jnp.clip(jnp.exp(math.log(0.12) - 1.7917595 * jax.random.uniform(splits[4], (NZ, NX, NY), jnp.float32) ** steps_of(splits[4], (NZ, NX, NY), ((0, 16),), -0.2, 0.2)), 0.02, 0.12)
    buoyancy = jnp.clip(1.0 + 0.1 * jax.random.normal(splits[5], (NZ, NX, NY), jnp.float32), 0.5, 1.5)
    traces = bell_draw(splits[6], (SHOTS, RECV, SAMPLES), 1.0, 6.0, ((0, 16), (1, 16)), jnp.float32)
    owner_slab_keys = jax.random.split(jax.random.fold_in(splits[7], 1), SHOTS * RECV // RB)
    owner_slab_turns = jax.random.permutation(jax.random.fold_in(splits[7], 3), SHOTS * RECV // RB)
    owner_slab = jax.vmap(lambda own, number: deal_out(jax.random.fold_in(splits[7], 2), own, number, RB, N_SLAB, 1, CAP, 2))(owner_slab_keys, owner_slab_turns).reshape((SHOTS, RECV, 1))
    depth_plane = touch_ends(jax.random.randint(splits[8], (SHOTS, RECV), 0, PLANES), jax.random.fold_in(splits[8], 1), 0, PLANES - 1).astype(jnp.int32)
    station_cell = touch_ends(jax.random.randint(splits[9], (SHOTS, RECV), 0, NX * NY), jax.random.fold_in(splits[9], 1), 0, (NX * NY) - 1).astype(jnp.int32)
    resampler = jnp.clip(jax.random.uniform(splits[10], (2, SAMPLES), jnp.float32, -3.0, 3.0), -3.0, 3.0)
    return {"pressure_old": pressure_old, "pressure_now": pressure_now, "adjoint_later": adjoint_later, "adjoint_now": adjoint_now, "stiffness": stiffness, "buoyancy": buoyancy, "traces": traces, "owner_slab": owner_slab, "depth_plane": depth_plane, "station_cell": station_cell, "resampler": resampler}


second_taps = (-205.0 / 72.0, 8.0 / 5.0, -1.0 / 5.0, 8.0 / 315.0, -1.0 / 560.0)
first_taps = (0.0, 4.0 / 5.0, -1.0 / 5.0, 4.0 / 105.0, -1.0 / 280.0)


def shifted(wavefield, offset, dimension):
    length = wavefield.shape[dimension]
    margin = abs(offset)
    shape_list = list(wavefield.shape)
    shape_list[dimension] = margin
    padding = jnp.zeros(tuple(shape_list), wavefield.dtype)
    if offset > 0:
        portion = lax.slice_in_dim(wavefield, margin, length, axis=dimension)
        return jnp.concatenate([portion, padding], axis=dimension)
    portion = lax.slice_in_dim(wavefield, 0, length - margin, axis=dimension)
    return jnp.concatenate([padding, portion], axis=dimension)


def derivatives(extended, planes):
    center = extended[4:4 + planes]
    second = (3.0 * second_taps[0]) * center
    slope_depth = jnp.zeros_like(center)
    slope_across = jnp.zeros_like(center)
    slope_along = jnp.zeros_like(center)
    for offset in range(1, 5):
        upward = extended[4 + offset:4 + offset + planes]
        downward = extended[4 - offset:4 - offset + planes]
        across_up = shifted(center, offset, 1)
        across_down = shifted(center, -offset, 1)
        along_up = shifted(center, offset, 2)
        along_down = shifted(center, -offset, 2)
        second = second + second_taps[offset] * (upward + downward + across_up + across_down + along_up + along_down)
        slope_depth = slope_depth + first_taps[offset] * (upward - downward)
        slope_across = slope_across + first_taps[offset] * (across_up - across_down)
        slope_along = slope_along + first_taps[offset] * (along_up - along_down)
    return second, slope_depth, slope_across, slope_along


def laplace_like(extended, buoyancy, slopes):
    second, slope_depth, slope_across, slope_along = derivatives(extended, buoyancy.shape[0])
    return buoyancy * second + slopes[0] * slope_depth + slopes[1] * slope_across + slopes[2] * slope_along


def deepen(wavefield):
    return jnp.pad(wavefield, ((4, 4), (0, 0), (0, 0)))


def reference(pressure_old, pressure_now, adjoint_later, adjoint_now, stiffness, buoyancy, traces, owner_slab, depth_plane, station_cell, resampler):
    slopes = derivatives(deepen(buoyancy), NZ)[1:]

    def operate(wavefield):
        return laplace_like(deepen(wavefield), buoyancy, slopes)

    def one_shot(total, items):
        old_field, now_field, later_field, adjoint_field, trace_rows, owners, planes_in, cells_in = items
        forward_one = 2.0 * now_field - old_field + stiffness * operate(now_field)
        forward_two = 2.0 * forward_one - now_field + stiffness * operate(forward_one)
        sources = jnp.dot(trace_rows, resampler.T, precision=lax.Precision.HIGHEST)
        cells = ((owners * PLANES + planes_in) * (NX * NY) + cells_in).astype(jnp.int32)
        inject_first = jnp.zeros((NZ * NX * NY,), jnp.float32).at[cells].add(sources[:, 0]).reshape(NZ, NX, NY)
        inject_second = jnp.zeros((NZ * NX * NY,), jnp.float32).at[cells].add(sources[:, 1]).reshape(NZ, NX, NY)
        adjoint_one = 2.0 * adjoint_field - later_field + stiffness * (operate(adjoint_field) + inject_first)
        adjoint_zero = 2.0 * adjoint_one - adjoint_field + stiffness * (operate(adjoint_one) + inject_second)
        term_first = adjoint_field * (forward_two - 2.0 * forward_one + now_field)
        term_second = adjoint_one * (forward_one - 2.0 * now_field + old_field)
        return total + (term_first + term_second), adjoint_zero

    gradient, adjoint_out = lax.scan(one_shot, jnp.zeros((NZ, NX, NY), jnp.float32), (pressure_old, pressure_now, adjoint_later, adjoint_now, traces, owner_slab[:, :, 0], depth_plane, station_cell))
    return gradient, adjoint_out
```

```python
import functools

import jax
import jax.numpy as jnp
import ml_dtypes
import numpy as np
from jax import lax
from jax.experimental import pallas as pl
from jax.experimental.pallas import tpu as pltpu
from jax.sharding import PartitionSpec as P

MESH = pl.DeviceIdType.MESH
F32 = jnp.float32
BF16 = jnp.bfloat16

SECOND = (-14350.0, 8064.0, -1008.0, 128.0, -9.0)
FIRST = (0.0, 672.0, -168.0, 32.0, -3.0)
LANES = 128
PAD = 8
HALO = 4
STEP = 4


def along_matrix():
    taps = np.zeros((LANES, 2 * LANES), np.float32)
    for m in range(1, 5):
        for j in range(LANES):
            if j + m < LANES:
                taps[j + m, j] = SECOND[m]
                taps[j + m, LANES + j] = FIRST[m]
            if j - m >= 0:
                taps[j - m, j] = SECOND[m]
                taps[j - m, LANES + j] = -FIRST[m]
    return np.concatenate([taps, taps], axis=0).astype(ml_dtypes.bfloat16)


def two_parts(v):
    high = v.astype(BF16)
    low = (v - high.astype(F32)).astype(BF16)
    return high, low


def three_parts(v):
    high = v.astype(BF16)
    rest = v - high.astype(F32)
    middle = rest.astype(BF16)
    low = (rest - middle.astype(F32)).astype(BF16)
    return high, middle, low


def iota(shape, dim):
    return lax.broadcasted_iota(jnp.int32, shape, dim)


def row_dot(a, b):
    return lax.dot_general(a, b, (((1,), (1,)), ((), ())), preferred_element_type=F32)


def kernel(
    n_shot,
    n_slab,
    planes,
    nx,
    rows,
    samples,
    old_in,
    now_in,
    later_in,
    adj_in,
    stiff_in,
    buoy_in,
    traces_in,
    owner_in,
    plane_in,
    cell_in,
    resample_in,
    along_in,
    grad_out,
    field_out,
    now,
    one,
    adj,
    aone,
    buoy,
    old,
    later,
    stiff,
    traces,
    owner,
    plane,
    cell,
    resample,
    along,
    cb,
    c0,
    c1,
    c2,
    term,
    inj,
    onto,
    part,
    rolled,
    mail,
    gsend,
    grecv,
    gsum,
    result,
    local_sem,
    halo_send,
    halo_recv,
    mail_send,
    mail_recv,
    grad_send,
    grad_recv,
    out_sem,
):
    shot = lax.axis_index("shot")
    slab = lax.axis_index("slab")
    groups = nx // 8
    blocks = planes // STEP
    cap = 2 * rows // n_slab
    per_tile = LANES // cap
    slots = n_slab * cap
    inner = pl.ds(PAD, nx)

    barrier = pltpu.get_barrier_semaphore()

    def greet_slab(k, carry):
        pl.semaphore_signal(
            barrier, inc=1, device_id={"slab": lax.rem(slab + k, n_slab)}, device_id_type=MESH
        )
        return carry

    def greet_shot(k, carry):
        pl.semaphore_signal(
            barrier, inc=1, device_id={"shot": lax.rem(shot + k, n_shot)}, device_id_type=MESH
        )
        return carry

    lax.fori_loop(1, n_slab, greet_slab, 0)
    lax.fori_loop(1, n_shot, greet_shot, 0)

    own = pl.ds(HALO, planes)
    local = [
        (traces_in.at[0], traces),
        (resample_in, resample),
        (owner_in, owner),
        (plane_in, plane),
        (cell_in, cell),
        (along_in, along),
        (buoy_in, buoy.at[own, inner]),
        (stiff_in, stiff),
        (now_in.at[0], now.at[own, inner]),
        (old_in.at[0], old),
        (adj_in.at[0], adj.at[own, inner]),
        (later_in.at[0], later),
    ]
    local = [pltpu.make_async_copy(s, d, local_sem.at[i]) for i, (s, d) in enumerate(local)]
    for copy in local:
        copy.start()

    pl.semaphore_wait(barrier, n_slab - 1 + n_shot - 1)

    top = pl.ds(planes, HALO)
    above = pl.ds(planes + HALO, HALO)
    first = pl.ds(HALO, HALO)
    below = pl.ds(0, HALO)

    def halo(i, low, high, field):
        down = pltpu.make_async_remote_copy(
            src_ref=low,
            dst_ref=field.at[above, inner],
            send_sem=halo_send.at[i, 0],
            recv_sem=halo_recv.at[i, 0],
            device_id={"slab": lax.max(slab - 1, 0)},
            device_id_type=MESH,
        )
        up = pltpu.make_async_remote_copy(
            src_ref=high,
            dst_ref=field.at[below, inner],
            send_sem=halo_send.at[i, 1],
            recv_sem=halo_recv.at[i, 1],
            device_id={"slab": lax.min(slab + 1, n_slab - 1)},
            device_id_type=MESH,
        )
        return down, up

    def halo_start(copies):
        @pl.when(slab > 0)
        def _():
            copies[0].start()

        @pl.when(slab < n_slab - 1)
        def _():
            copies[1].start()

    def halo_arrive(copies):
        @pl.when(slab < n_slab - 1)
        def _():
            copies[0].wait_recv()

        @pl.when(slab > 0)
        def _():
            copies[1].wait_recv()

    def halo_sent(copies):
        @pl.when(slab > 0)
        def _():
            copies[0].wait_send()

        @pl.when(slab < n_slab - 1)
        def _():
            copies[1].wait_send()

    low_in, high_in = pl.ds(0, HALO), pl.ds(planes - HALO, HALO)
    halo_now = halo(0, now_in.at[0, low_in], now_in.at[0, high_in], now)
    halo_buoy = halo(1, buoy_in.at[low_in], buoy_in.at[high_in], buoy)
    halo_adj = halo(2, adj_in.at[0, low_in], adj_in.at[0, high_in], adj)
    halo_one = halo(3, one.at[first, inner], one.at[top, inner], one)
    halo_aone = halo(4, aone.at[first, inner], aone.at[top, inner], aone)
    halo_start(halo_now)
    halo_start(halo_buoy)
    halo_start(halo_adj)

    edge = jnp.zeros((PAD, LANES), F32)

    def clear(z, carry):
        for field in (now, one, adj, aone, buoy):
            field[HALO + z, pl.ds(0, PAD)] = edge
            field[HALO + z, pl.ds(PAD + nx, PAD)] = edge
        return carry

    lax.fori_loop(0, planes, clear, 0)
    outside = jnp.zeros((HALO, nx, LANES), F32)

    @pl.when(slab == 0)
    def _():
        for field in (now, one, adj, aone, buoy):
            field[below, inner] = outside

    @pl.when(slab == n_slab - 1)
    def _():
        for field in (now, one, adj, aone, buoy):
            field[above, inner] = outside

    for copy in local[:5]:
        copy.wait()

    def resampled(i, carry):
        at = pl.ds(pl.multiple_of(i * 32, 32), 32)
        sums = [jnp.zeros((32, LANES), F32)] * 2
        for k in range(samples // LANES):
            lanes = pl.ds(k * LANES, LANES)
            rows_of = traces[at, lanes]
            for j in range(2):
                sums[j] = sums[j] + rows_of * resample[pl.ds(j, 1), lanes]
        for j in range(2):
            part[j, at] = sums[j]
        return carry

    lax.fori_loop(0, rows // 32, resampled, 0)
    ones = jnp.ones((16, LANES), BF16)
    pieces = []
    for j in range(2):
        source = sum(row_dot(ones, piece) for piece in three_parts(part[j]))
        pieces += three_parts(source)

    owners = owner[...]
    member = jnp.where(iota((n_slab, rows), 0) == owners, 1.0, 0.0)
    earlier = jnp.where(iota((rows, rows), 0) < iota((rows, rows), 1), 1.0, 0.0)
    count = jnp.dot(member.astype(BF16), earlier.astype(BF16), preferred_element_type=F32)
    rank = jnp.sum(member * count, axis=0, keepdims=True).astype(jnp.int32)
    target = owners * cap + rank
    place = jnp.where(iota((slots, rows), 0) == target, 1.0, 0.0).astype(BF16)
    cells = cell[...]
    pieces += [
        plane[...].astype(F32),
        (cells // LANES).astype(F32),
        (cells % LANES).astype(F32),
    ]
    table = jnp.zeros((16, rows), F32)
    line = iota((16, rows), 0)
    for i, piece in enumerate(pieces):
        table = jnp.where(line == i, piece.astype(F32), table)
    sorted_rows = row_dot(table.astype(BF16), place)

    def sorted_row(i):
        return sorted_rows[i : i + 1]

    letter = jnp.zeros((8, slots), F32)
    line = iota((8, slots), 0)
    letter_rows = [
        sorted_row(0) + sorted_row(1) + sorted_row(2),
        sorted_row(3) + sorted_row(4) + sorted_row(5),
        sorted_row(6) * float(nx) + sorted_row(7),
        sorted_row(8),
    ]
    for i, letter_row in enumerate(letter_rows):
        letter = jnp.where(line == i, letter_row, letter)
    mine = iota((8, LANES), 1) // cap == lax.rem(slab, per_tile)
    for j in range(per_tile):
        for t in range(slots // LANES):
            tile = letter[:, t * LANES : (t + 1) * LANES]
            if j:
                tile = pltpu.roll(tile, j * cap, 1)
            rolled[j, t] = jnp.where(mine, tile, 0.0)

    def mail_copy(k):
        to = lax.rem(slab + k, n_slab)
        return pltpu.make_async_remote_copy(
            src_ref=rolled.at[lax.rem(n_slab - k, per_tile), to // per_tile],
            dst_ref=mail.at[k],
            send_sem=mail_send.at[k],
            recv_sem=mail_recv.at[k],
            device_id={"slab": to},
            device_id_type=MESH,
        )

    def mail_start(k, carry):
        mail_copy(k).start()
        return carry

    lax.fori_loop(1, n_slab, mail_start, 0)
    mail[0] = rolled[0, slab // per_tile]

    weights = along

    def along_lines(field, at):
        lines = jnp.concatenate([field[at + p, inner] for p in range(STEP)], axis=0)
        return jnp.dot(
            jnp.concatenate(two_parts(lines), axis=1), weights[...], preferred_element_type=F32
        )

    def stencil(field, block, need_second, finish):
        at = HALO + block * STEP
        lines = along_lines(field, at)
        for g in range(groups):
            lo = PAD + 8 * g
            column = [field[at - HALO + q, pl.ds(lo, 8)] for q in range(STEP + 2 * HALO)]
            finished = []
            for p in range(STEP):
                centre = column[HALO + p]
                here = p * nx + 8 * g
                second = None
                if need_second:
                    second = 3.0 * SECOND[0] * centre + lines[here : here + 8, :LANES]
                depth = across = None
                for m in range(1, 5):
                    up, down = column[HALO + p + m], column[HALO + p - m]
                    right = field[at + p, pl.ds(lo + m, 8)]
                    left = field[at + p, pl.ds(lo - m, 8)]
                    if need_second:
                        second = second + SECOND[m] * ((up + down) + (right + left))
                    d, a = FIRST[m] * (up - down), FIRST[m] * (right - left)
                    depth = d if depth is None else depth + d
                    across = a if across is None else across + a
                slopes = (depth, across, lines[here : here + 8, LANES:])
                finished.append(
                    finish(block * STEP + p, pl.ds(8 * g, 8), pl.ds(lo, 8), centre, second, slopes)
                )
            if finished[0] is not None:
                exchange(block, g, finished)

    def waves(field, block, finish):
        def close(z, at, at_padded, centre, second, slopes):
            change = (
                cb[z, at] * second
                + c0[z, at] * slopes[0]
                + c1[z, at] * slopes[1]
                + c2[z, at] * slopes[2]
            )
            return finish(z, at, at_padded, centre, change)

        stencil(field, block, True, close)

    line8 = iota((8, LANES), 0)
    half = line8 < 4
    even = (line8 // 2) % 2 == 0

    def exchange(block, g, v):
        a = [jnp.where(half, v[p], pltpu.roll(v[p + 2], 4, 0)) for p in range(2)]
        b = [jnp.where(half, pltpu.roll(v[p], 4, 0), v[p + 2]) for p in range(2)]
        at = pl.ds(pl.multiple_of(block * 8, 8), 8)
        for i, (c, d) in enumerate((a, b)):
            gsend[4 * g + 2 * i, at] = jnp.where(even, c, pltpu.roll(d, 2, 0))
            gsend[4 * g + 2 * i + 1, at] = jnp.where(even, pltpu.roll(c, 6, 0), d)

    def model_block(block):
        def close(z, at, at_padded, centre, second, slopes):
            k = stiff[z, at]
            cb[z, at] = k * centre * (1.0 / 5040.0)
            k = k * (1.0 / (840.0 * 840.0))
            c0[z, at] = k * slopes[0]
            c1[z, at] = k * slopes[1]
            c2[z, at] = k * slopes[2]

        stencil(buoy, block, False, close)

    def forward_one(block):
        def close(z, at, at_padded, centre, change):
            one[HALO + z, at_padded] = (centre + centre) - old[z, at] + change
            term[z, at] = change

        waves(now, block, close)

    def lines_of(z, at):
        return pl.ds(pl.multiple_of(z * nx + at.start, 8), 8)

    def adjoint_one(block):
        def close(z, at, at_padded, centre, change):
            injected = stiff[z, at] * inj[lines_of(z, at), pl.ds(0, LANES)]
            value = (centre + centre) - later[z, at] + (change + injected)
            aone[HALO + z, at_padded] = value
            term[z, at] = value * term[z, at]

        waves(adj, block, close)

    def gradient(block):
        def close(z, at, at_padded, centre, change):
            return term[z, at] + adj[HALO + z, at_padded] * change

        waves(one, block, close)

    def adjoint_two(block):
        def close(z, at, at_padded, centre, change):
            injected = stiff[z, at] * inj[lines_of(z, at), pl.ds(LANES, LANES)]
            result[z, at] = (
                (centre + centre) - adj[HALO + z, at_padded] + (change + injected)
            )

        waves(aone, block, close)

    def middle(work):
        def body(block, carry):
            work(block)
            return carry

        lax.fori_loop(1, blocks - 1, body, 0)

    def ends(work):
        def body(i, carry):
            work(i * (blocks - 1))
            return carry

        lax.fori_loop(0, 2, body, 0)

    for copy in local[5:10]:
        copy.wait()
    middle(model_block)
    middle(forward_one)
    halo_arrive(halo_buoy)
    halo_arrive(halo_now)
    ends(model_block)
    ends(forward_one)
    halo_start(halo_one)

    def mail_arrive(k, carry):
        mail_copy(k).wait_recv()
        return carry

    lax.fori_loop(1, n_slab, mail_arrive, 0)
    letters = jnp.concatenate(
        [
            sum(mail[q * per_tile + k] for k in range(per_tile))
            for q in range(n_slab // per_tile)
        ],
        axis=1,
    )
    cell_y = letters[3:4].astype(jnp.int32)
    cell_zx = letters[2:3].astype(jnp.int32)
    hit = iota((LANES, slots), 0) == cell_y
    spread = jnp.concatenate(
        [jnp.where(hit, letters[j : j + 1], 0.0) for j in range(2)], axis=0
    ).T
    high, low = two_parts(spread)
    onto[pl.ds(0, slots)] = high
    onto[pl.ds(slots, slots)] = low
    chunk = 4 * nx

    def inject(i, carry):
        base = i * chunk
        pick = jnp.where(iota((chunk, slots), 0) + base == cell_zx, 1.0, 0.0).astype(BF16)
        inj[pl.ds(pl.multiple_of(base, chunk), chunk)] = jnp.dot(
            jnp.concatenate([pick, pick], axis=1), onto[...], preferred_element_type=F32
        )
        return carry

    lax.fori_loop(0, planes * nx // chunk, inject, 0)

    for copy in local[10:]:
        copy.wait()
    halo_arrive(halo_adj)
    ends(adjoint_one)
    halo_start(halo_aone)
    middle(adjoint_one)

    spans = ((8, 8 * (blocks - 2)), (0, 8), (8 * (blocks - 1), 8))

    def grad_copy(c, k):
        to = lax.rem(shot + k, n_shot)
        at = pl.ds(*spans[c])
        return pltpu.make_async_remote_copy(
            src_ref=gsend.at[to, at],
            dst_ref=grecv.at[k, at],
            send_sem=grad_send.at[c, k],
            recv_sem=grad_recv.at[c, k],
            device_id={"shot": to},
            device_id_type=MESH,
        )

    def grad_start(chunks):
        def body(k, carry):
            for c in chunks:
                grad_copy(c, k).start()
            return carry

        lax.fori_loop(1, n_shot, body, 0)

    middle(gradient)
    grad_start((0,))
    halo_arrive(halo_one)
    ends(gradient)
    grad_start((1, 2))

    middle(adjoint_two)
    halo_arrive(halo_aone)
    ends(adjoint_two)
    field_copy = pltpu.make_async_copy(result, field_out, out_sem.at[0])
    field_copy.start()

    def grad_arrive(k, carry):
        for c in range(3):
            grad_copy(c, k).wait_recv()
        return carry

    lax.fori_loop(1, n_shot, grad_arrive, 0)
    gsum[...] = gsend[shot] + sum(grecv[k] for k in range(1, n_shot))
    grad_write = pltpu.make_async_copy(gsum, grad_out, out_sem.at[1])
    grad_write.start()

    for copies in (halo_now, halo_buoy, halo_adj, halo_one, halo_aone):
        halo_sent(copies)

    def mail_sent(k, carry):
        mail_copy(k).wait_send()
        return carry

    lax.fori_loop(1, n_slab, mail_sent, 0)

    def grad_sent(k, carry):
        for c in range(3):
            grad_copy(c, k).wait_send()
        return carry

    lax.fori_loop(1, n_shot, grad_sent, 0)
    field_copy.wait()
    grad_write.wait()


def on_device(
    pressure_old,
    pressure_now,
    adjoint_later,
    adjoint_now,
    stiffness,
    buoyancy,
    traces,
    owner_slab,
    depth_plane,
    station_cell,
    resampler,
):
    n_shot, n_slab = lax.axis_size("shot"), lax.axis_size("slab")
    planes, nx, _ = buoyancy.shape
    rows, samples = traces.shape[1:]
    slots = 2 * rows
    own_rows = planes * (nx // n_shot)
    padded = pltpu.VMEM((planes + 2 * HALO, nx + 2 * PAD, LANES), F32)
    plain = pltpu.VMEM((planes, nx, LANES), F32)
    dma = pltpu.SemaphoreType.DMA
    grad, field = pl.pallas_call(
        functools.partial(kernel, n_shot, n_slab, planes, nx, rows, samples),
        name="imaging",
        out_shape=(
            jax.ShapeDtypeStruct((own_rows, LANES), F32),
            jax.ShapeDtypeStruct((planes, nx, LANES), F32),
        ),
        in_specs=[pl.BlockSpec(memory_space=pl.ANY)] * 12,
        out_specs=(pl.BlockSpec(memory_space=pl.ANY),) * 2,
        scratch_shapes=[
            padded,
            padded,
            padded,
            padded,
            padded,
            plain,
            plain,
            plain,
            pltpu.VMEM((rows, samples), F32),
            pltpu.VMEM((1, rows), jnp.int32),
            pltpu.VMEM((1, rows), jnp.int32),
            pltpu.VMEM((1, rows), jnp.int32),
            pltpu.VMEM((2, samples), F32),
            pltpu.VMEM((2 * LANES, 2 * LANES), BF16),
            plain,
            plain,
            plain,
            plain,
            plain,
            pltpu.VMEM((planes * nx, 2 * LANES), F32),
            pltpu.VMEM((2 * slots, 2 * LANES), BF16),
            pltpu.VMEM((2, rows, LANES), F32),
            pltpu.VMEM((LANES * n_slab // slots, slots // LANES, 8, LANES), F32),
            pltpu.VMEM((n_slab, 8, LANES), F32),
            pltpu.VMEM((n_shot, own_rows, LANES), F32),
            pltpu.VMEM((n_shot, own_rows, LANES), F32),
            pltpu.VMEM((own_rows, LANES), F32),
            plain,
            dma((12,)),
            dma((5, 2)),
            dma((5, 2)),
            dma((n_slab,)),
            dma((n_slab,)),
            dma((3, n_shot)),
            dma((3, n_shot)),
            dma((2,)),
        ],
        compiler_params=pltpu.CompilerParams(
            collective_id=0, has_side_effects=True, vmem_limit_bytes=56 * 1024 * 1024
        ),
    )(
        pressure_old,
        pressure_now,
        adjoint_later,
        adjoint_now,
        stiffness,
        buoyancy,
        traces,
        owner_slab.reshape(1, rows),
        depth_plane,
        station_cell,
        resampler,
        jnp.asarray(along_matrix()),
    )
    return grad.reshape(planes, nx // n_shot, LANES), field[None]


def solution(mesh):
    return jax.shard_map(
        on_device,
        mesh=mesh,
        in_specs=(
            P("shot", "slab", None, None),
            P("shot", "slab", None, None),
            P("shot", "slab", None, None),
            P("shot", "slab", None, None),
            P("slab", None, None),
            P("slab", None, None),
            P("shot", "slab", None),
            P("shot", "slab", None),
            P("shot", "slab"),
            P("shot", "slab"),
            P(),
        ),
        out_specs=(P("slab", "shot", None), P("shot", "slab", None, None)),
        check_vma=False,
    )
```

```python
import functools

import jax
import jax.numpy as jnp
import ml_dtypes
import numpy as np
from jax import lax
from jax.experimental import pallas as pl
from jax.experimental.pallas import tpu as pltpu
from jax.sharding import PartitionSpec as P

MESH = pl.DeviceIdType.MESH
F32 = jnp.float32
BF16 = jnp.bfloat16

SECOND = (-14350.0, 8064.0, -1008.0, 128.0, -9.0)
FIRST = (0.0, 672.0, -168.0, 32.0, -3.0)
LANES = 128
PAD = 8
HALO = 4
STEP = 4


def along_matrix():
    taps = np.zeros((LANES, 2 * LANES), np.float32)
    for m in range(1, 5):
        for j in range(LANES):
            if j + m < LANES:
                taps[j + m, j] = SECOND[m]
                taps[j + m, LANES + j] = FIRST[m]
            if j - m >= 0:
                taps[j - m, j] = SECOND[m]
                taps[j - m, LANES + j] = -FIRST[m]
    return np.concatenate([taps, taps], axis=0).astype(ml_dtypes.bfloat16)


def two_parts(v):
    high = v.astype(BF16)
    low = (v - high.astype(F32)).astype(BF16)
    return high, low


def three_parts(v):
    high = v.astype(BF16)
    rest = v - high.astype(F32)
    middle = rest.astype(BF16)
    low = (rest - middle.astype(F32)).astype(BF16)
    return high, middle, low


def iota(shape, dim):
    return lax.broadcasted_iota(jnp.int32, shape, dim)


def row_dot(a, b):
    return lax.dot_general(a, b, (((1,), (1,)), ((), ())), preferred_element_type=F32)


def kernel(
    n_shot,
    n_slab,
    planes,
    nx,
    rows,
    samples,
    old_in,
    now_in,
    later_in,
    adj_in,
    stiff_in,
    buoy_in,
    traces_in,
    owner_in,
    plane_in,
    cell_in,
    resample_in,
    along_in,
    grad_out,
    field_out,
    now,
    one,
    adj,
    aone,
    buoy,
    old,
    later,
    stiff,
    traces,
    owner,
    plane,
    cell,
    resample,
    along,
    cb,
    c0,
    c1,
    c2,
    term,
    inj,
    onto,
    part,
    rolled,
    mail,
    gsend,
    grecv,
    lines_a,
    lines_b,
    lines_c,
    lines_d,
    local_sem,
    halo_send,
    halo_recv,
    mail_send,
    mail_recv,
    grad_send,
    grad_recv,
):
    shot = lax.axis_index("shot")
    slab = lax.axis_index("slab")
    groups = nx // 8
    blocks = planes // STEP
    cap = 2 * rows // n_slab
    per_tile = LANES // cap
    slots = n_slab * cap
    inner = pl.ds(PAD, nx)
    even_lines, odd_lines = (lines_a, lines_b), (lines_c, lines_d)

    barrier = pltpu.get_barrier_semaphore()

    own = pl.ds(HALO, planes)
    local = [
        (buoy_in, buoy.at[own, inner]),
        (stiff_in, stiff),
        (along_in, along),
        (traces_in.at[0], traces),
        (resample_in, resample),
        (owner_in, owner),
        (plane_in, plane),
        (cell_in, cell),
        (now_in.at[0], now.at[own, inner]),
        (old_in.at[0], old),
        (adj_in.at[0], adj.at[own, inner]),
        (later_in.at[0], later),
    ]
    local = [pltpu.make_async_copy(s, d, local_sem.at[i]) for i, (s, d) in enumerate(local)]
    for copy in local[:3]:
        copy.start()

    def greet_slab(k, carry):
        pl.semaphore_signal(
            barrier, inc=1, device_id={"slab": lax.rem(slab + k, n_slab)}, device_id_type=MESH
        )
        return carry

    def greet_shot(k, carry):
        pl.semaphore_signal(
            barrier, inc=1, device_id={"shot": lax.rem(shot + k, n_shot)}, device_id_type=MESH
        )
        return carry

    lax.fori_loop(1, n_slab, greet_slab, 0)
    lax.fori_loop(1, n_shot, greet_shot, 0)

    for copy in local[3:]:
        copy.start()

    top = pl.ds(planes, HALO)
    above = pl.ds(planes + HALO, HALO)
    first = pl.ds(HALO, HALO)
    below = pl.ds(0, HALO)

    def halo(i, low, high, field):
        down = pltpu.make_async_remote_copy(
            src_ref=low,
            dst_ref=field.at[above, inner],
            send_sem=halo_send.at[i, 0],
            recv_sem=halo_recv.at[i, 0],
            device_id={"slab": lax.max(slab - 1, 0)},
            device_id_type=MESH,
        )
        up = pltpu.make_async_remote_copy(
            src_ref=high,
            dst_ref=field.at[below, inner],
            send_sem=halo_send.at[i, 1],
            recv_sem=halo_recv.at[i, 1],
            device_id={"slab": lax.min(slab + 1, n_slab - 1)},
            device_id_type=MESH,
        )
        return down, up

    def halo_start(copies):
        @pl.when(slab > 0)
        def _():
            copies[0].start()

        @pl.when(slab < n_slab - 1)
        def _():
            copies[1].start()

    def halo_arrive(copies):
        @pl.when(slab < n_slab - 1)
        def _():
            copies[0].wait_recv()

        @pl.when(slab > 0)
        def _():
            copies[1].wait_recv()

    def halo_sent(copies):
        @pl.when(slab > 0)
        def _():
            copies[0].wait_send()

        @pl.when(slab < n_slab - 1)
        def _():
            copies[1].wait_send()

    low_in, high_in = pl.ds(0, HALO), pl.ds(planes - HALO, HALO)
    halo_now = halo(0, now_in.at[0, low_in], now_in.at[0, high_in], now)
    halo_buoy = halo(1, buoy_in.at[low_in], buoy_in.at[high_in], buoy)
    halo_adj = halo(2, adj_in.at[0, low_in], adj_in.at[0, high_in], adj)
    halo_one = halo(3, one.at[first, inner], one.at[top, inner], one)
    halo_aone = halo(4, aone.at[first, inner], aone.at[top, inner], aone)
    edge = jnp.zeros((PAD, LANES), F32)

    def clear(z, carry):
        for field in (now, one, adj, aone, buoy):
            field[HALO + z, pl.ds(0, PAD)] = edge
            field[HALO + z, pl.ds(PAD + nx, PAD)] = edge
        return carry

    lax.fori_loop(0, planes, clear, 0)
    outside = jnp.zeros((HALO, nx, LANES), F32)

    @pl.when(slab == 0)
    def _():
        for field in (now, one, adj, aone, buoy):
            field[below, inner] = outside

    @pl.when(slab == n_slab - 1)
    def _():
        for field in (now, one, adj, aone, buoy):
            field[above, inner] = outside

    def fill(field, block, lines):
        at = HALO + block * STEP
        whole = jnp.concatenate([field[at + p, inner] for p in range(STEP)], axis=0)
        lines[...] = jnp.dot(
            jnp.concatenate(two_parts(whole), axis=1), along[...], preferred_element_type=F32
        )

    def stencil(field, block, lines, need_second, finish):
        at = HALO + block * STEP
        for g in range(groups):
            lo = PAD + 8 * g
            column = [field[at - HALO + q, pl.ds(lo, 8)] for q in range(STEP + 2 * HALO)]
            finished = []
            for p in range(STEP):
                centre = column[HALO + p]
                here = p * nx + 8 * g
                second = None
                if need_second:
                    second = 3.0 * SECOND[0] * centre + lines[here : here + 8, :LANES]
                depth = across = None
                for m in range(1, 5):
                    up, down = column[HALO + p + m], column[HALO + p - m]
                    right = field[at + p, pl.ds(lo + m, 8)]
                    left = field[at + p, pl.ds(lo - m, 8)]
                    if need_second:
                        second = second + SECOND[m] * ((up + down) + (right + left))
                    d, a = FIRST[m] * (up - down), FIRST[m] * (right - left)
                    depth = d if depth is None else depth + d
                    across = a if across is None else across + a
                slopes = (depth, across, lines[here : here + 8, LANES:])
                finished.append(
                    finish(block * STEP + p, pl.ds(8 * g, 8), pl.ds(lo, 8), centre, second, slopes)
                )
            if finished[0] is not None:
                exchange(block, g, finished)

    def waves(field, block, lines, finish):
        def close(z, at, at_padded, centre, second, slopes):
            change = (
                cb[z, at] * second
                + c0[z, at] * slopes[0]
                + c1[z, at] * slopes[1]
                + c2[z, at] * slopes[2]
            )
            return finish(z, at, at_padded, centre, change)

        stencil(field, block, lines, True, close)

    line8 = iota((8, LANES), 0)
    half = line8 < 4
    even = (line8 // 2) % 2 == 0

    def exchange(block, g, v):
        a = [jnp.where(half, v[p], pltpu.roll(v[p + 2], 4, 0)) for p in range(2)]
        b = [jnp.where(half, pltpu.roll(v[p], 4, 0), v[p + 2]) for p in range(2)]
        at = pl.ds(pl.multiple_of(block * 8, 8), 8)
        for i, (c, d) in enumerate((a, b)):
            gsend[4 * g + 2 * i, at] = jnp.where(even, c, pltpu.roll(d, 2, 0))
            gsend[4 * g + 2 * i + 1, at] = jnp.where(even, pltpu.roll(c, 6, 0), d)

    def model_block(block, lines):
        def close(z, at, at_padded, centre, second, slopes):
            k = stiff[z, at]
            cb[z, at] = k * centre * (1.0 / 5040.0)
            k = k * (1.0 / (840.0 * 840.0))
            c0[z, at] = k * slopes[0]
            c1[z, at] = k * slopes[1]
            c2[z, at] = k * slopes[2]

        stencil(buoy, block, lines, False, close)

    def forward_one(block, lines):
        def close(z, at, at_padded, centre, change):
            one[HALO + z, at_padded] = (centre + centre) - old[z, at] + change
            term[z, at] = change

        waves(now, block, lines, close)

    def lines_of(z, at):
        return pl.ds(pl.multiple_of(z * nx + at.start, 8), 8)

    def adjoint_one(block, lines):
        def close(z, at, at_padded, centre, change):
            injected = stiff[z, at] * inj[lines_of(z, at), pl.ds(0, LANES)]
            value = (centre + centre) - later[z, at] + (change + injected)
            aone[HALO + z, at_padded] = value
            term[z, at] = value * term[z, at]

        waves(adj, block, lines, close)

    def gradient(block, lines):
        def close(z, at, at_padded, centre, change):
            return term[z, at] + adj[HALO + z, at_padded] * change

        waves(one, block, lines, close)

    def adjoint_two(block, lines):
        def close(z, at, at_padded, centre, change):
            injected = stiff[z, at] * inj[lines_of(z, at), pl.ds(LANES, LANES)]
            field_out[z, at] = (
                (centre + centre) - adj[HALO + z, at_padded] + (change + injected)
            )

        waves(aone, block, lines, close)

    def middle(works, begin, end, fresh=True):
        if fresh:
            for j, (field, work) in enumerate(works):
                fill(field, 1 + 2 * begin, even_lines[j])

        def body(i, carry):
            block = 1 + 2 * i
            for j, (field, work) in enumerate(works):
                fill(field, block + 1, odd_lines[j])
            for j, (field, work) in enumerate(works):
                work(block, even_lines[j])
            for j, (field, work) in enumerate(works):
                fill(field, block + 2, even_lines[j])
            for j, (field, work) in enumerate(works):
                work(block + 1, odd_lines[j])
            return carry

        lax.fori_loop(begin, end, body, 0)

    def ends(field, work):
        fill(field, 0, even_lines[0])
        fill(field, blocks - 1, odd_lines[0])
        work(0, even_lines[0])
        work(blocks - 1, odd_lines[0])

    pairs = (blocks - 2) // 2
    for copy in local[:3]:
        copy.wait()
    middle(((buoy, model_block),), 0, pairs)

    pl.semaphore_wait(barrier, n_slab - 1 + n_shot - 1)
    halo_start(halo_now)
    halo_start(halo_buoy)
    halo_start(halo_adj)

    for copy in local[3:8]:
        copy.wait()

    def resampled(i, carry):
        at = pl.ds(pl.multiple_of(i * 32, 32), 32)
        sums = [jnp.zeros((32, LANES), F32)] * 2
        for k in range(samples // LANES):
            lanes = pl.ds(k * LANES, LANES)
            rows_of = traces[at, lanes]
            for j in range(2):
                sums[j] = sums[j] + rows_of * resample[pl.ds(j, 1), lanes]
        for j in range(2):
            part[j, at] = sums[j]
        return carry

    lax.fori_loop(0, rows // 32, resampled, 0)
    ones = jnp.ones((16, LANES), BF16)
    pieces = []
    for j in range(2):
        source = sum(row_dot(ones, piece) for piece in three_parts(part[j]))
        pieces += three_parts(source)

    owners = owner[...]
    member = jnp.where(iota((n_slab, rows), 0) == owners, 1.0, 0.0)
    earlier = jnp.where(iota((rows, rows), 0) < iota((rows, rows), 1), 1.0, 0.0)
    count = jnp.dot(member.astype(BF16), earlier.astype(BF16), preferred_element_type=F32)
    rank = jnp.sum(member * count, axis=0, keepdims=True).astype(jnp.int32)
    target = owners * cap + rank
    place = jnp.where(iota((slots, rows), 0) == target, 1.0, 0.0).astype(BF16)
    cells = cell[...]
    pieces += [
        plane[...].astype(F32),
        (cells // LANES).astype(F32),
        (cells % LANES).astype(F32),
    ]
    table = jnp.zeros((16, rows), F32)
    line = iota((16, rows), 0)
    for i, piece in enumerate(pieces):
        table = jnp.where(line == i, piece.astype(F32), table)
    sorted_rows = row_dot(table.astype(BF16), place)

    def sorted_row(i):
        return sorted_rows[i : i + 1]

    letter = jnp.zeros((8, slots), F32)
    line = iota((8, slots), 0)
    letter_rows = [
        sorted_row(0) + sorted_row(1) + sorted_row(2),
        sorted_row(3) + sorted_row(4) + sorted_row(5),
        sorted_row(6) * float(nx) + sorted_row(7),
        sorted_row(8),
    ]
    for i, letter_row in enumerate(letter_rows):
        letter = jnp.where(line == i, letter_row, letter)
    mine = iota((8, LANES), 1) // cap == lax.rem(slab, per_tile)
    for j in range(per_tile):
        for t in range(slots // LANES):
            tile = letter[:, t * LANES : (t + 1) * LANES]
            if j:
                tile = pltpu.roll(tile, j * cap, 1)
            rolled[j, t] = jnp.where(mine, tile, 0.0)

    def mail_copy(k):
        to = lax.rem(slab + k, n_slab)
        return pltpu.make_async_remote_copy(
            src_ref=rolled.at[lax.rem(n_slab - k, per_tile), to // per_tile],
            dst_ref=mail.at[k],
            send_sem=mail_send.at[k],
            recv_sem=mail_recv.at[k],
            device_id={"slab": to},
            device_id_type=MESH,
        )

    def mail_start(k, carry):
        mail_copy(k).start()
        return carry

    lax.fori_loop(1, n_slab, mail_start, 0)
    mail[0] = rolled[0, slab // per_tile]

    for copy in local[8:10]:
        copy.wait()
    middle(((now, forward_one),), 0, pairs)
    halo_arrive(halo_buoy)
    halo_arrive(halo_now)
    ends(buoy, model_block)
    ends(now, forward_one)
    halo_start(halo_one)

    def mail_arrive(k, carry):
        mail_copy(k).wait_recv()
        return carry

    lax.fori_loop(1, n_slab, mail_arrive, 0)
    letters = jnp.concatenate(
        [
            sum(mail[q * per_tile + k] for k in range(per_tile))
            for q in range(n_slab // per_tile)
        ],
        axis=1,
    )
    cell_y = letters[3:4].astype(jnp.int32)
    cell_zx = letters[2:3].astype(jnp.int32)
    hit = iota((LANES, slots), 0) == cell_y
    spread = jnp.concatenate(
        [jnp.where(hit, letters[j : j + 1], 0.0) for j in range(2)], axis=0
    ).T
    high, low = two_parts(spread)
    onto[pl.ds(0, slots)] = high
    onto[pl.ds(slots, slots)] = low
    chunk = planes * nx // 4

    def inject(i, carry):
        base = i * chunk
        pick = jnp.where(iota((chunk, slots), 0) + base == cell_zx, 1.0, 0.0).astype(BF16)
        inj[pl.ds(pl.multiple_of(base, chunk), chunk)] = jnp.dot(
            jnp.concatenate([pick, pick], axis=1), onto[...], preferred_element_type=F32
        )
        return carry

    lax.fori_loop(0, 4, inject, 0)

    for copy in local[10:]:
        copy.wait()
    halo_arrive(halo_adj)
    ends(adj, adjoint_one)
    halo_start(halo_aone)

    parts = (0, pairs // 2, pairs)
    spans = [(8 + 16 * lo, 16 * (hi - lo)) for lo, hi in zip(parts, parts[1:])]
    spans += [(0, 8), (8 * (blocks - 1), 8)]

    def grad_copy(c, k):
        to = lax.rem(shot + k, n_shot)
        at = pl.ds(*spans[c])
        return pltpu.make_async_remote_copy(
            src_ref=gsend.at[to, at],
            dst_ref=grecv.at[k, at],
            send_sem=grad_send.at[c, k],
            recv_sem=grad_recv.at[c, k],
            device_id={"shot": to},
            device_id_type=MESH,
        )

    def grad_start(chunks):
        def body(k, carry):
            for c in chunks:
                grad_copy(c, k).start()
            return carry

        lax.fori_loop(1, n_shot, body, 0)

    both = ((adj, adjoint_one), (one, gradient))
    for c in range(2):
        middle(both, parts[c], parts[c + 1], fresh=c == 0)
        grad_start((c,))
    halo_arrive(halo_one)
    ends(one, gradient)
    grad_start((2, 3))

    middle(((aone, adjoint_two),), 0, pairs)
    halo_arrive(halo_aone)
    ends(aone, adjoint_two)

    def grad_arrive(k, carry):
        for c in range(len(spans)):
            grad_copy(c, k).wait_recv()
        return carry

    lax.fori_loop(1, n_shot, grad_arrive, 0)
    grad_out[...] = gsend[shot] + sum(grecv[k] for k in range(1, n_shot))

    for copies in (halo_now, halo_buoy, halo_adj, halo_one, halo_aone):
        halo_sent(copies)

    def mail_sent(k, carry):
        mail_copy(k).wait_send()
        return carry

    lax.fori_loop(1, n_slab, mail_sent, 0)

    def grad_sent(k, carry):
        for c in range(len(spans)):
            grad_copy(c, k).wait_send()
        return carry

    lax.fori_loop(1, n_shot, grad_sent, 0)


def hand_on(grad_in, field_in, grad_out, field_out, sem):
    grad_copy = pltpu.make_async_copy(grad_in, grad_out, sem.at[0])
    field_copy = pltpu.make_async_copy(field_in, field_out, sem.at[1])
    grad_copy.start()
    field_copy.start()
    grad_copy.wait()
    field_copy.wait()


def on_device(
    pressure_old,
    pressure_now,
    adjoint_later,
    adjoint_now,
    stiffness,
    buoyancy,
    traces,
    owner_slab,
    depth_plane,
    station_cell,
    resampler,
):
    n_shot, n_slab = lax.axis_size("shot"), lax.axis_size("slab")
    planes, nx, _ = buoyancy.shape
    rows, samples = traces.shape[1:]
    slots = 2 * rows
    own_rows = planes * (nx // n_shot)
    padded = pltpu.VMEM((planes + 2 * HALO, nx + 2 * PAD, LANES), F32)
    plain = pltpu.VMEM((planes, nx, LANES), F32)
    dma = pltpu.SemaphoreType.DMA
    grad, field = pl.pallas_call(
        functools.partial(kernel, n_shot, n_slab, planes, nx, rows, samples),
        name="imaging",
        out_shape=(
            pltpu.VMEM((own_rows, LANES), F32),
            pltpu.VMEM((planes, nx, LANES), F32),
        ),
        in_specs=[pl.BlockSpec(memory_space=pltpu.HBM)] * 12,
        out_specs=(pl.BlockSpec(memory_space=pltpu.VMEM),) * 2,
        scratch_shapes=[
            padded,
            padded,
            padded,
            padded,
            padded,
            plain,
            plain,
            plain,
            pltpu.VMEM((rows, samples), F32),
            pltpu.VMEM((1, rows), jnp.int32),
            pltpu.VMEM((1, rows), jnp.int32),
            pltpu.VMEM((1, rows), jnp.int32),
            pltpu.VMEM((2, samples), F32),
            pltpu.VMEM((2 * LANES, 2 * LANES), BF16),
            plain,
            plain,
            plain,
            plain,
            plain,
            pltpu.VMEM((planes * nx, 2 * LANES), F32),
            pltpu.VMEM((2 * slots, 2 * LANES), BF16),
            pltpu.VMEM((2, rows, LANES), F32),
            pltpu.VMEM((LANES * n_slab // slots, slots // LANES, 8, LANES), F32),
            pltpu.VMEM((n_slab, 8, LANES), F32),
            pltpu.VMEM((n_shot, own_rows, LANES), F32),
            pltpu.VMEM((n_shot, own_rows, LANES), F32),
            *[pltpu.VMEM((STEP * nx, 2 * LANES), F32)] * 4,
            dma((12,)),
            dma((5, 2)),
            dma((5, 2)),
            dma((n_slab,)),
            dma((n_slab,)),
            dma((4, n_shot)),
            dma((4, n_shot)),
        ],
        compiler_params=pltpu.CompilerParams(
            collective_id=0, has_side_effects=True, vmem_limit_bytes=61 * 1024 * 1024
        ),
    )(
        pressure_old,
        pressure_now,
        adjoint_later,
        adjoint_now,
        stiffness,
        buoyancy,
        traces,
        owner_slab.reshape(1, rows),
        depth_plane,
        station_cell,
        resampler,
        jnp.asarray(along_matrix()),
    )
    grad, field = pl.pallas_call(
        hand_on,
        name="hand_on",
        out_shape=(
            jax.ShapeDtypeStruct((own_rows, LANES), F32),
            jax.ShapeDtypeStruct((planes, nx, LANES), F32),
        ),
        in_specs=[pl.BlockSpec(memory_space=pl.ANY)] * 2,
        out_specs=(pl.BlockSpec(memory_space=pltpu.HBM),) * 2,
        scratch_shapes=[dma((2,))],
        compiler_params=pltpu.CompilerParams(vmem_limit_bytes=1024 * 1024),
    )(grad, field)
    return grad.reshape(planes, nx // n_shot, LANES), field[None]


def solution(mesh):
    return jax.shard_map(
        on_device,
        mesh=mesh,
        in_specs=(
            P("shot", "slab", None, None),
            P("shot", "slab", None, None),
            P("shot", "slab", None, None),
            P("shot", "slab", None, None),
            P("slab", None, None),
            P("slab", None, None),
            P("shot", "slab", None),
            P("shot", "slab", None),
            P("shot", "slab"),
            P("shot", "slab"),
            P(),
        ),
        out_specs=(P("slab", "shot", None), P("shot", "slab", None, None)),
        check_vma=False,
    )
```
